32 devices in a mesh: ctx: 16 (over z, y, core), tp: 2 (over x).
Axes of the slice: x: 2, y: 2, z: 4, core: 2. Of those that a mesh axis runs over, the one named last changes fastest.
Arguments:
- pre_queries: bfloat16 [2048, 16384], P('ctx', 'tp'), may hold values from -90 to 90
- pre_keys: bfloat16 [2048, 1024], P('ctx', 'tp'), may hold values from -4.5 to 4.5
- pre_values: bfloat16 [2048, 1024], P('ctx', 'tp'), may hold values from -6 to 6
- block_pos: int32 [32], P('ctx'), may hold values from 0 to 31, each once
- block_dest: int32 [32, 1], P('ctx'), may hold values from 0 to 15; in each aligned block of 32 rows (0 to 31, 32 to 63, ...) at most 4 rows name the same one
- dec_queries: bfloat16 [32, 4, 16384], P('ctx'), may hold values from -90 to 90
- new_keys: bfloat16 [32, 4, 1024], P('ctx', None, 'tp'), may hold values from -4.5 to 4.5
- new_values: bfloat16 [32, 4, 1024], P('ctx', None, 'tp'), may hold values from -6 to 6
- cache_keys: bfloat16 [32, 2048, 1024], P('ctx', 'tp'), may hold values from -6 to 6
- cache_values: bfloat16 [32, 2048, 1024], P('ctx', 'tp'), may hold values from -6 to 6
- cache_len: int32 [32], P('ctx'), may hold values from 1 to 2048, 32768 in all
Outputs:
- prefill_out: bfloat16 [2048, 16384], P('ctx', 'tp')
- decode_out: bfloat16 [32, 4, 16384], P('ctx', None, 'tp')
The draws below stay inside these ranges and needn't reach their ends.
Inputs may be any that keep to these rules, and one draw needn't show every extreme that they name: `block_pos`: each of the 2 * 16 half-block positions appears once. `block_dest`: no decode index is named by more than 4 half-blocks, a bound that some block reaches. `cache_len`: some row has exactly 2048 live positions.
All inputs are finite; a program needn't handle non-finite values. No bound on the sum of `cache_len` on one device may be relied on, other than what follows from the above.
Results may differ from the reference program's by a relative error of at most 0.0065.
Values may be sent and summed in bfloat16 or wider, within the bound.
A program may use at most 192 MiB of HBM per device.

```python
import math
import jax
import jax.numpy as jnp
import numpy as np
from jax import lax

QH = 128
KVH = 8
HD = 128
TOK_DEV = 128
TOKENS = 2048
DROWS = 2
ROWS = 32
CACHE_DEV = 1024
CACHE = 2048
STEPS = 4
MOST = 4
N_CTX = 16


def prefill_pair(key):
    key = jax.random.fold_in(key, 11)
    subkeys = jax.random.split(key, 2)
    group_size = QH // KVH
    fresh_keys = jnp.clip(jax.random.normal(subkeys[0], (TOKENS, KVH, HD), jnp.float32), -4.5, 4.5)
    queries = jnp.clip(jax.random.normal(subkeys[1], (TOKENS, KVH, group_size, HD), jnp.float32), -4.5, 4.5)
    return (fresh_keys, queries)


def decode_pair(key):
    key = jax.random.fold_in(key, 12)
    subkeys = jax.random.split(key, 2)
    group_size = QH // KVH
    fresh_keys = jnp.clip(jax.random.normal(subkeys[0], (ROWS, STEPS, KVH, HD), jnp.float32), -4.5, 4.5)
    queries = jnp.clip(jax.random.normal(subkeys[1], (ROWS, STEPS, KVH, group_size, HD), jnp.float32), -4.5, 4.5)
    return (fresh_keys, queries)


def draw_pre_queries(key, part):
    fresh_keys, queries = prefill_pair(key)
    return queries.reshape(TOKENS, QH * HD).astype(jnp.bfloat16)


def draw_pre_keys(key, part):
    fresh_keys, queries = prefill_pair(key)
    return fresh_keys.reshape(TOKENS, KVH * HD).astype(jnp.bfloat16)


def draw_dec_queries(key, part):
    fresh_keys, queries = decode_pair(key)
    return queries.reshape(ROWS, STEPS, QH * HD).astype(jnp.bfloat16)


def draw_new_keys(key, part):
    fresh_keys, queries = decode_pair(key)
    return fresh_keys.reshape(ROWS, STEPS, KVH * HD).astype(jnp.bfloat16)


def draw_cache_keys(key, part):
    key = jax.random.fold_in(key, 13)
    subkeys = jax.random.split(key, 1)
    shard_total = CACHE // CACHE_DEV
    stored = jnp.clip(jax.random.normal(subkeys[0], (ROWS, shard_total, CACHE_DEV, KVH, HD), jnp.float32), -6.0, 6.0)
    first = stored[:, :, 0]
    stored = stored.at[:, :, 0].set(first)
    return stored.reshape(ROWS, CACHE, KVH * HD).astype(jnp.bfloat16)


def level_of(rng, shape, pieces, low, largest):
    gain, own = 1.0, jax.random.fold_in(rng, 6)
    for axis_at, shards_of in pieces:
        draws = jnp.exp(jax.random.uniform(jax.random.fold_in(own, axis_at), (shards_of,), jnp.float32, low / len(pieces), largest / len(pieces)))
        gain = gain * jnp.repeat(draws, shape[axis_at] // shards_of).reshape([-1 if axis == axis_at else 1 for axis in range(len(shape))])
    return gain


def length_profile(amount, total, most, lean):
    weights = [(1 << 20) // math.isqrt(standing ** lean) + 1 for standing in range(2, amount + 1)]
    spare, given = total - most - (amount - 1), [1] * (amount - 1)
    while spare > 0:
        movable = [i for i in range(amount - 1) if given[i] < most]
        mass, left = sum([weights[i] for i in movable]), spare
        for i in movable:
            extra = min(most - given[i], max(1, left * weights[i] // mass), spare)
            given[i] = given[i] + extra
            spare = spare - extra
    return np.array([most] + given)


def ragged(own_key, number_of, total, bound, lean):
    if number_of == 2:
        one = jax.random.randint(own_key, (), max(1, total - bound), min(bound, total - 1) + 1)
        return jnp.stack([one, total - one])
    sizes = jnp.asarray(length_profile(number_of, total, bound, lean), jnp.int32)
    twos = (number_of - 1) // 2
    donor, receiver = sizes[1:1 + 2 * twos:2], sizes[2:2 + 2 * twos:2]
    slack = jnp.minimum(donor - 1, bound - receiver)
    shifted = jax.random.randint(jax.random.fold_in(own_key, 1), (twos,), 0, 1 << 20) % (slack + 1)
    sizes = sizes.at[1:1 + 2 * twos:2].set(donor - shifted).at[2:2 + 2 * twos:2].set(receiver + shifted)
    return sizes[jax.random.permutation(jax.random.fold_in(own_key, 2), number_of)]


def assign_block(rng, own, number, rows, amount, top, limit, lean):
    sequence = jax.random.permutation(rng, amount)
    crowded, usual = shares(amount, rows * top, limit, lean, True), shares(amount, rows * top, limit, lean, False)
    places = jnp.arange(amount)

    def named(tallies, turn):
        used = int((tallies > 0).sum())
        fixed = max(1, used // 4)
        shifted = fixed + (places - fixed + turn * (used - fixed)) % max(1, amount - fixed)
        return jnp.zeros((amount,), jnp.int32).at[sequence[jnp.where(places < fixed, places, shifted)]].set(jnp.asarray(tallies, jnp.int32))

    tallies = jnp.where(number % 4 == 0, named(crowded, number // 4), named(usual, number - number // 4 - 1))
    mixed = jax.random.permutation(jax.random.fold_in(own, 3), amount)
    donor, receiver = mixed[0:amount // 2 * 2:2], mixed[1:amount // 2 * 2:2]
    slack = jnp.minimum(tallies[donor] - 1, limit - tallies[receiver]) // 2
    slack = jnp.where((donor == sequence[0]) | (receiver == sequence[0]) | (tallies[receiver] == 0), 0, jnp.maximum(slack, 0))
    shifted = jax.random.randint(jax.random.fold_in(own, 4), (amount // 2,), 0, 1 << 20) % (slack + 1)
    tallies = tallies.at[donor].add(-shifted).at[receiver].add(shifted)
    labels = jnp.searchsorted(jnp.cumsum(tallies), jnp.arange(rows * top), side="right").astype(jnp.int32)
    table = labels.reshape(top, rows).T
    table = table[jax.random.permutation(jax.random.fold_in(own, 1), rows)]
    turn = jax.random.randint(jax.random.fold_in(own, 2), (rows, 1), 0, top)
    return jnp.take_along_axis(table, (jnp.arange(top)[None, :] + turn) % top, axis=1)


def shares(count, total, most, skew, full):
    portions = [(1 << 20) // math.isqrt(standing ** skew) + 1 for standing in range(1, count + 1)]
    largest = most if full else min(most, max(-(-total // count), total * portions[0] // sum(portions)))
    least = 1 if total - largest >= count - 1 else 0
    counts, spare = [largest] + [least] * (count - 1), total - largest - least * (count - 1)
    while spare > 0:
        movable = [i for i in range(1, count) if counts[i] < largest] or [i for i in range(1, count) if counts[i] < most]
        whole, remaining = sum([portions[i] for i in movable]), spare
        for i in movable:
            addition = min(most - counts[i], max(1, remaining * portions[i] // whole), spare)
            counts[i] = counts[i] + addition
            spare = spare - addition
    return np.array(counts)


def bell_draw(key, extent, deviation, bound, pieces=(), kind=jnp.bfloat16):
    loudness = level_of(key, extent, pieces, -0.22, 0.18) if pieces else 1.0
    values = jax.random.normal(key, extent, jnp.float32) * deviation * loudness
    return jnp.minimum(jnp.maximum(values, -bound), bound).astype(kind)


def setup_inputs(seed: int = 0) -> dict:
    key_list = jax.random.split(jax.random.key(seed), 12)
    pre_queries = draw_pre_queries(jax.random.fold_in(key_list[11], 71), 0)
    pre_keys = draw_pre_keys(jax.random.fold_in(key_list[11], 71), 0)
    pre_values = bell_draw(key_list[2], (TOKENS, KVH * HD), 1.0, 6.0, ((0, 16), (1, 2)))
    block_pos = jax.random.permutation(key_list[3], 2 * N_CTX).astype(jnp.int32)
    block_dest_keys = jax.random.split(jax.random.fold_in(key_list[4], 1), (2 * N_CTX) // (2 * N_CTX))
    block_dest_turns = jax.random.permutation(jax.random.fold_in(key_list[4], 3), (2 * N_CTX) // (2 * N_CTX))
    block_dest = jax.vmap(lambda own, number: assign_block(jax.random.fold_in(key_list[4], 2), own, number, 2 * N_CTX, N_CTX, 1, MOST, 2))(block_dest_keys, block_dest_turns).reshape((2 * N_CTX, 1))
    dec_queries = draw_dec_queries(jax.random.fold_in(key_list[11], 71), 0)
    new_keys = draw_new_keys(jax.random.fold_in(key_list[11], 71), 0)
    new_values = bell_draw(key_list[7], (ROWS, STEPS, KVH * HD), 1.0, 6.0, ((0, 16), (2, 2)))
    cache_keys = draw_cache_keys(jax.random.fold_in(key_list[11], 71), 0)
    cache_values = bell_draw(key_list[9], (ROWS, CACHE, KVH * HD), 1.0, 6.0, ((0, 16), (1, 2)))
    cache_len = ragged(key_list[10], ROWS, ROWS * CACHE // 2, CACHE, 2).astype(jnp.int32)
    return dict(pre_queries=pre_queries, pre_keys=pre_keys, pre_values=pre_values, block_pos=block_pos, block_dest=block_dest, dec_queries=dec_queries, new_keys=new_keys, new_values=new_values, cache_keys=cache_keys, cache_values=cache_values, cache_len=cache_len)


def token_positions(starts, half_len):
    offsets = jnp.arange(half_len, dtype=jnp.int32)
    return (starts[:, None] * half_len + offsets[None, :]).reshape(-1)

def reference(pre_queries, pre_keys, pre_values, block_pos, block_dest, dec_queries, new_keys, new_values, cache_keys, cache_values, cache_len):
    half_len = TOK_DEV // 2
    group_size = QH // KVH
    inv_root = 1.0 / math.sqrt(HD)
    positions = token_positions(block_pos, half_len)
    visible = positions[None, :] <= positions[:, None]
    head_queries = pre_queries.reshape(TOKENS, QH, HD).transpose(1, 0, 2)
    head_keys = pre_keys.reshape(TOKENS, KVH, HD).transpose(1, 0, 2)
    head_values = pre_values.reshape(TOKENS, KVH, HD).transpose(1, 0, 2)

    def prefill_head(head_index):
        kv_index = head_index // group_size
        scores = jnp.dot(head_queries[head_index], head_keys[kv_index].T, preferred_element_type=jnp.float32) * inv_root
        scores = jnp.where(visible, scores, -jnp.inf)
        weights = jnp.exp(scores - scores.max(axis=-1, keepdims=True))
        totals = weights.sum(axis=-1, keepdims=True)
        mixed = jnp.dot(weights.astype(jnp.bfloat16), head_values[kv_index], preferred_element_type=jnp.float32) / totals
        return mixed.astype(jnp.bfloat16)
    prefill_heads = lax.map(prefill_head, jnp.arange(QH, dtype=jnp.int32))
    prefill_out = prefill_heads.transpose(1, 0, 2).reshape(TOKENS, QH * HD)
    token_dest = jnp.repeat(block_dest[:, 0], half_len)
    flat_keys = pre_keys.reshape(TOKENS, KVH, HD)
    flat_values = pre_values.reshape(TOKENS, KVH, HD)
    step_order = jnp.arange(STEPS, dtype=jnp.int32)
    causal_new = step_order[None, :] <= step_order[:, None]
    cache_pos = jnp.arange(CACHE, dtype=jnp.int32)

    def decode_row(row_index):
        owner = (row_index // DROWS).astype(jnp.int32)
        row_queries = dec_queries[row_index].reshape(STEPS, KVH, group_size, HD).astype(jnp.float32)
        row_keys = jnp.concatenate([flat_keys, cache_keys[row_index].reshape(CACHE, KVH, HD), new_keys[row_index].reshape(STEPS, KVH, HD)], axis=0).astype(jnp.float32)
        row_values = jnp.concatenate([flat_values, cache_values[row_index].reshape(CACHE, KVH, HD), new_values[row_index].reshape(STEPS, KVH, HD)], axis=0).astype(jnp.float32)
        live_old = jnp.concatenate([token_dest == owner, cache_pos < cache_len[row_index]], axis=0)
        live = jnp.concatenate([jnp.broadcast_to(live_old[None, :], (STEPS, TOKENS + CACHE)), causal_new], axis=1)
        scores = jnp.einsum('skgd,ukd->skgu', row_queries, row_keys) * inv_root
        scores = jnp.where(live[:, None, None, :], scores, -jnp.inf)
        weights = jnp.exp(scores - scores.max(axis=-1, keepdims=True))
        totals = weights.sum(axis=-1)
        rounded = lax.optimization_barrier(weights.astype(jnp.bfloat16)).astype(jnp.float32)
        mixed = jnp.einsum('skgu,ukd->skgd', rounded, row_values) / totals[..., None]
        return mixed.reshape(STEPS, QH * HD).astype(jnp.bfloat16)
    decode_out = lax.map(decode_row, jnp.arange(ROWS, dtype=jnp.int32))
    return (prefill_out, decode_out)
```

```python
import functools
import math

import jax
import jax.numpy as jnp
from jax import lax
from jax.experimental import pallas as pl
from jax.experimental.pallas import tpu as pltpu
from jax.sharding import PartitionSpec as P

QH = 128
KVH = 8
HD = 128
GROUP = QH // KVH
FILL = -1e30
C2 = math.log2(math.e) / math.sqrt(HD)
META = 16
HEADS_STEP = 4
NT = (((1,), (1,)), ((), ()))


def lanes(index, width=HD):
    return pl.ds(pl.multiple_of(index * width, HD), width)


def softmax_tile(scores, bias, old):
    width = scores.shape[1] // HD
    parts = [scores[:, c * HD : (c + 1) * HD] * C2 + bias(c) for c in range(width)]
    top = functools.reduce(jnp.maximum, parts)
    peak = jnp.broadcast_to(jnp.max(top, axis=-1, keepdims=True), top.shape)
    fade = None
    if old is not None:
        peak = jnp.maximum(peak, old)
        fade = jnp.exp2(old - peak)
    parts = [jnp.exp2(part - peak) for part in parts]
    total = functools.reduce(jnp.add, parts)
    weights = jnp.concatenate([part.astype(jnp.bfloat16) for part in parts], axis=1)
    return peak, fade, total, weights


def kernel(
    n_ctx,
    n_tp,
    pos_ref,
    len_ref,
    load_ref,
    q_ref,
    dq_ref,
    fresh_ref,
    ck_hbm,
    cv_hbm,
    out_ref,
    dec_ref,
    slots,
    peak_ref,
    total_ref,
    acc_ref,
    bias_ref,
    dbias_ref,
    ck,
    cv,
    cst,
    rx,
    ring_send,
    ring_recv,
    sib_send,
    sib_recv,
    tp_send,
    tp_recv,
    cache_sem,
):
    tok = q_ref.shape[0]
    half_len = tok // 2
    hd = load_ref.shape[1] // HD
    heads = hd * GROUP
    rows = ck.shape[0]
    cache_dev = ck.shape[1]
    per_row = dq_ref.shape[1] // rows
    n_chip = n_ctx // 2
    half = n_chip // 2

    me = lax.axis_index("ctx")
    tp = lax.axis_index("tp")
    chip, core = lax.div(me, 2), lax.rem(me, 2)
    sibling = me + 1 - 2 * core
    line, along = lax.rem(chip, 2), lax.div(chip, 2)
    place = along + line * (n_chip - 1 - 2 * along)

    def chip_at(position):
        position = lax.rem(position + 2 * n_chip, n_chip)
        far = lax.div(position, half)
        return 2 * (position + far * (n_chip - 1 - 2 * position)) + far

    def owner(position):
        return chip_at(position) * 2 + core

    def sib_owner(position):
        return chip_at(position) * 2 + 1 - core

    right, left = owner(place + 1), owner(place - 1)

    cache_copies = []
    for r in range(rows):
        pair = []
        for which, (src, dst) in enumerate(((ck_hbm, ck), (cv_hbm, cv))):
            copy = pltpu.make_async_copy(src.at[r], dst.at[r], cache_sem.at[r, which])
            copy.start()
            pair.append(copy)
        cache_copies.append(pair)

    barrier = pltpu.get_barrier_semaphore()
    for other in (right, left, sibling):
        pl.semaphore_signal(
            barrier, inc=1, device_id={"ctx": other}, device_id_type=pl.DeviceIdType.MESH
        )
    for d in range(1, n_tp):
        pl.semaphore_signal(
            barrier,
            inc=1,
            device_id={"tp": lax.rem(tp + d, n_tp)},
            device_id_type=pl.DeviceIdType.MESH,
        )
    pl.semaphore_wait(barrier, 3 + n_tp - 1)

    def ring_copy(way, step, src, slot, part):
        dst = slots.at[slot] if part is None else slots.at[slot, part]
        return pltpu.make_async_remote_copy(
            src_ref=dst if src is None else src,
            dst_ref=dst,
            send_sem=ring_send.at[way, step],
            recv_sem=ring_recv.at[way, step],
            device_id={"ctx": left if way else right},
            device_id_type=pl.DeviceIdType.MESH,
        )

    def sib_copy(way, step, src, slot):
        dst = slots.at[slot]
        return pltpu.make_async_remote_copy(
            src_ref=dst if src is None else src,
            dst_ref=dst,
            send_sem=sib_send.at[way, step],
            recv_sem=sib_recv.at[way, step],
            device_id={"ctx": sibling},
            device_id_type=pl.DeviceIdType.MESH,
        )

    first_part, second_part = pl.ds(0, tok + META), pl.ds(tok + META, tok)
    sent = []

    def start(copy):
        copy.start()
        sent.append(copy)

    def part_of(way, step):
        if step < half:
            return None
        return second_part if way else first_part

    start(ring_copy(0, 1, load_ref, me, None))
    start(ring_copy(1, 1, load_ref, me, None))
    start(sib_copy(0, 0, load_ref, me))

    def ring_arrive(step):
        slot = [owner(place - step), owner(place + step)]
        for way in (0, 1):
            ring_copy(way, step, None, slot[way], part_of(way, step)).wait_recv()
            if step < half:
                start(ring_copy(way, step + 1, None, slot[way], part_of(way, step + 1)))
        if step < half:
            start(sib_copy(0, step, None, slot[0]))
            start(sib_copy(1, step, None, slot[1]))
            return [slots.at[slot[0]], slots.at[slot[1]]]
        start(sib_copy(0, step, None, slot[0]))
        return [slots.at[slot[0]]]

    def sib_arrive(step):
        slot = [sib_owner(place - step), sib_owner(place + step)]
        ways = (0, 1) if 0 < step < half else (0,)
        for way in ways:
            sib_copy(way, step, None, slot[way]).wait_recv()
        return [slots.at[slot[way]] for way in ways]

    row = lax.broadcasted_iota(jnp.int32, (tok, HD), 0)
    lane = lax.broadcasted_iota(jnp.int32, (tok, HD), 1)
    own_pos = jnp.where(row < half_len, pos_ref[0], pos_ref[1]) * half_len + lax.rem(row, half_len)
    own_pos = own_pos.astype(jnp.float32)
    lane_off = lax.rem(lane, half_len).astype(jnp.float32)
    me_f = me.astype(jnp.float32)

    def chunk(blocks, first, last):
        width = len(blocks)
        for c, block in enumerate(blocks):
            meta = block[tok : tok + META, 0:HD].astype(jnp.float32)
            key_pos = meta[0:1, :] * float(half_len) + lane_off
            bias_ref[c] = jnp.where(key_pos <= own_pos, 0.0, FILL)
            dbias_ref[c] = jnp.where(jnp.broadcast_to(meta[1:2, :], (tok, HD)) == me_f, 0.0, FILL)

        def keys_values(k):
            keys = jnp.concatenate([b[0:tok, lanes(k)] for b in blocks], axis=0)
            values = jnp.concatenate([b[tok + META : 2 * tok + META, lanes(k)] for b in blocks], axis=0)
            return keys, values

        def body(i, _):
            base = i * HEADS_STEP
            keys, values = keys_values(lax.div(base, GROUP))
            queries = jnp.concatenate([q_ref[:, lanes(base + j)] for j in range(HEADS_STEP)], axis=0)
            scores = lax.dot_general(queries, keys, NT, preferred_element_type=jnp.float32)
            weights, totals, fades = [], [], []
            for j in range(HEADS_STEP):
                old = None if first else peak_ref[base + j]
                peak, fade, total, weight = softmax_tile(
                    scores[j * tok : (j + 1) * tok], lambda c: bias_ref[c], old
                )
                if not first:
                    total = total + total_ref[base + j] * fade
                if not last:
                    peak_ref[base + j] = peak
                    total_ref[base + j] = total
                weights.append(weight)
                totals.append(total)
                fades.append(fade)
            mixed = jnp.dot(
                jnp.concatenate(weights, axis=0), values, preferred_element_type=jnp.float32
            )
            for j in range(HEADS_STEP):
                acc = mixed[j * tok : (j + 1) * tok]
                if not first:
                    acc = acc + acc_ref[base + j] * fades[j]
                if last:
                    whole = jnp.sum(totals[j], axis=-1, keepdims=True)
                    out_ref[:, lanes(base + j)] = (acc / whole).astype(jnp.bfloat16)
                else:
                    acc_ref[base + j] = acc
            return 0

        lax.fori_loop(0, heads // HEADS_STEP, body, 0)

        def dec_body(k, _):
            keys, values = keys_values(k)
            dec_step(k, keys, values, lambda c: dbias_ref[c], False)
            return 0

        lax.fori_loop(0, hd, dec_body, 0)

    def dec_step(k, keys, values, bias, first):
        at = heads + k
        scores = lax.dot_general(
            dq_ref[tp * hd + k], keys, NT, preferred_element_type=jnp.float32
        )
        old = None if first else peak_ref[at]
        peak, fade, total, weight = softmax_tile(scores, bias, old)
        acc = jnp.dot(weight, values, preferred_element_type=jnp.float32)
        if not first:
            total = total + total_ref[at] * fade
            acc = acc + acc_ref[at] * fade
        peak_ref[at] = peak
        total_ref[at] = total
        acc_ref[at] = acc

    drow = lax.broadcasted_iota(jnp.int32, (rows * per_row, HD), 0)
    dlane = lax.broadcasted_iota(jnp.int32, (rows * per_row, HD), 1)
    steps = per_row // GROUP
    fresh_live = (lax.div(drow, per_row) == lax.div(dlane, steps)) & (
        lax.rem(dlane, steps) <= lax.rem(drow, steps)
    )
    dbias_ref[0] = jnp.where(fresh_live, 0.0, FILL)

    def fresh_body(k, _):
        dec_step(k, fresh_ref[0, :, lanes(k)], fresh_ref[1, :, lanes(k)], lambda c: dbias_ref[0], True)
        return 0

    lax.fori_loop(0, hd, fresh_body, 0)

    chunk([load_ref] + sib_arrive(0), True, False)

    crow = lax.broadcasted_iota(jnp.int32, (per_row, HD), 1)
    for r in range(rows):
        for copy in cache_copies[r]:
            copy.wait()

        def cache_body(k, _):
            queries = dq_ref[k, r * per_row : (r + 1) * per_row, :]
            scores = lax.dot_general(
                queries, ck[r, :, lanes(k)], NT, preferred_element_type=jnp.float32
            )
            limit = len_ref[r] - tp * cache_dev
            peak, _, total, weight = softmax_tile(
                scores, lambda c: jnp.where(crow + c * HD < limit, 0.0, FILL), None
            )
            acc = jnp.dot(weight, cv[r, :, lanes(k)], preferred_element_type=jnp.float32)
            whole = jnp.broadcast_to(jnp.sum(total, axis=-1, keepdims=True), total.shape)
            cst[k, 0, r * per_row : (r + 1) * per_row, :] = acc
            cst[k, 1, r * per_row : (r + 1) * per_row, :] = jnp.where(crow < HD // 2, peak, whole)
            return 0

        lax.fori_loop(0, KVH, cache_body, 0)

    def tp_copy(d):
        other = lax.rem(tp + d, n_tp)
        return pltpu.make_async_remote_copy(
            src_ref=cst.at[pl.ds(other * hd, hd)],
            dst_ref=rx.at[d],
            send_sem=tp_send.at[d],
            recv_sem=tp_recv.at[d],
            device_id={"tp": other},
            device_id_type=pl.DeviceIdType.MESH,
        )

    tp_copies = [tp_copy(d) for d in range(1, n_tp)]
    for copy in tp_copies:
        copy.start()

    arrived = ring_arrive(1)
    chunk(arrived, False, False)
    for step in range(2, half):
        arrived = ring_arrive(step)
        chunk(sib_arrive(step - 1) + arrived, False, False)
    arrived = ring_arrive(half)
    chunk(sib_arrive(half - 1), False, False)
    chunk(arrived + sib_arrive(half), False, True)

    for copy in tp_copies:
        copy.wait_recv()

    def final_body(k, _):
        at = heads + k
        peak, acc = peak_ref[at], acc_ref[at]
        whole = jnp.broadcast_to(jnp.sum(total_ref[at], axis=-1, keepdims=True), acc.shape)
        for d in range(n_tp):
            if d == 0:
                part, stats = cst[tp * hd + k, 0], cst[tp * hd + k, 1]
            else:
                part, stats = rx[d, k, 0], rx[d, k, 1]
            far_peak = jnp.broadcast_to(stats[:, 0:1], acc.shape)
            far_whole = jnp.broadcast_to(stats[:, HD // 2 : HD // 2 + 1], acc.shape)
            top = jnp.maximum(peak, far_peak)
            fade, far_fade = jnp.exp2(peak - top), jnp.exp2(far_peak - top)
            whole = whole * fade + far_whole * far_fade
            acc = acc * fade + part * far_fade
            peak = top
        dec_ref[k] = (acc / whole).astype(jnp.bfloat16)
        return 0

    lax.fori_loop(0, hd, final_body, 0)
    for copy in sent:
        copy.wait_send()
    for copy in tp_copies:
        copy.wait_send()


def per_device(
    n_ctx,
    n_tp,
    pre_queries,
    pre_keys,
    pre_values,
    block_pos,
    block_dest,
    dec_queries,
    new_keys,
    new_values,
    cache_keys,
    cache_values,
    cache_len,
):
    tok, width = pre_keys.shape
    hd = width // HD
    rows, steps = dec_queries.shape[:2]
    cache_dev = cache_keys.shape[1]
    dec_all = rows * steps * GROUP
    half = n_ctx // 4
    half_len = tok // 2

    marks = jnp.stack([jnp.repeat(block_pos, half_len), jnp.repeat(block_dest[:, 0], half_len)])
    marks = jnp.pad(marks.astype(jnp.bfloat16), ((0, META - 2), (0, width - tok)))
    load = jnp.concatenate([pre_keys, marks, pre_values], axis=0)
    dq = dec_queries.reshape(rows, steps, KVH, GROUP, HD).transpose(2, 0, 3, 1, 4)
    dq = dq.reshape(KVH, dec_all, HD)
    fresh = jnp.stack([new_keys, new_values]).reshape(2, rows * steps, width)
    fresh = jnp.pad(fresh, ((0, 0), (0, HD - rows * steps), (0, 0)))

    vmem = pl.BlockSpec(memory_space=pltpu.VMEM)
    smem = pl.BlockSpec(memory_space=pltpu.SMEM)
    hbm = pl.BlockSpec(memory_space=pl.ANY)
    states = hd * GROUP + hd
    out, dec = pl.pallas_call(
        functools.partial(kernel, n_ctx, n_tp),
        out_shape=(
            jax.ShapeDtypeStruct((tok, hd * GROUP * HD), jnp.bfloat16),
            jax.ShapeDtypeStruct((hd, dec_all, HD), jnp.bfloat16),
        ),
        in_specs=[smem, smem, vmem, vmem, vmem, vmem, hbm, hbm],
        out_specs=(vmem, vmem),
        scratch_shapes=[
            pltpu.VMEM((n_ctx, 2 * tok + META, width), jnp.bfloat16),
            pltpu.VMEM((states, tok, HD), jnp.float32),
            pltpu.VMEM((states, tok, HD), jnp.float32),
            pltpu.VMEM((states, tok, HD), jnp.float32),
            pltpu.VMEM((4, tok, HD), jnp.float32),
            pltpu.VMEM((4, dec_all, HD), jnp.float32),
            pltpu.VMEM((rows, cache_dev, KVH * HD), jnp.bfloat16),
            pltpu.VMEM((rows, cache_dev, KVH * HD), jnp.bfloat16),
            pltpu.VMEM((KVH, 2, dec_all, HD), jnp.float32),
            pltpu.VMEM((n_tp, hd, 2, dec_all, HD), jnp.float32),
            pltpu.SemaphoreType.DMA((2, half + 1)),
            pltpu.SemaphoreType.DMA((2, half + 1)),
            pltpu.SemaphoreType.DMA((2, half + 1)),
            pltpu.SemaphoreType.DMA((2, half + 1)),
            pltpu.SemaphoreType.DMA((n_tp,)),
            pltpu.SemaphoreType.DMA((n_tp,)),
            pltpu.SemaphoreType.DMA((rows, 2)),
        ],
        compiler_params=pltpu.CompilerParams(
            collective_id=0, has_side_effects=True, vmem_limit_bytes=56 * 1024 * 1024
        ),
    )(block_pos, cache_len, load, pre_queries, dq, fresh, cache_keys, cache_values)
    dec = dec.reshape(hd, rows, GROUP, steps, HD).transpose(1, 3, 0, 2, 4)
    return out, dec.reshape(rows, steps, hd * GROUP * HD)


def solution(mesh):
    placed = (
        P("ctx", "tp"),
        P("ctx", "tp"),
        P("ctx", "tp"),
        P("ctx"),
        P("ctx", None),
        P("ctx", None, None),
        P("ctx", None, "tp"),
        P("ctx", None, "tp"),
        P("ctx", "tp", None),
        P("ctx", "tp", None),
        P("ctx"),
    )
    return jax.shard_map(
        functools.partial(per_device, mesh.shape["ctx"], mesh.shape["tp"]),
        mesh=mesh,
        in_specs=placed,
        out_specs=(P("ctx", "tp"), P("ctx", None, "tp")),
        check_vma=False,
    )
```

```python
import functools
import math

import jax
import jax.numpy as jnp
from jax import lax
from jax.experimental import pallas as pl
from jax.experimental.pallas import tpu as pltpu
from jax.sharding import PartitionSpec as P

QH = 128
KVH = 8
HD = 128
GROUP = QH // KVH
FILL = -1e30
C2 = math.log2(math.e) / math.sqrt(HD)
META = 16
HEADS_STEP = 8
NT = (((1,), (1,)), ((), ()))


def lanes(index, width=HD):
    return pl.ds(pl.multiple_of(index * width, HD), width)


def softmax_tile(scores, bias, old):
    width = scores.shape[1] // HD
    parts = [scores[:, c * HD : (c + 1) * HD] * C2 + bias(c) for c in range(width)]
    top = functools.reduce(jnp.maximum, parts)
    peak = jnp.broadcast_to(jnp.max(top, axis=-1, keepdims=True), top.shape)
    fade = None
    if old is not None:
        peak = jnp.maximum(peak, old)
        fade = jnp.exp2(old - peak)
    parts = [jnp.exp2(part - peak) for part in parts]
    total = functools.reduce(jnp.add, parts)
    weights = jnp.concatenate([part.astype(jnp.bfloat16) for part in parts], axis=1)
    return peak, fade, total, weights


def kernel(
    n_ctx,
    n_tp,
    pos_ref,
    dest_ref,
    len_ref,
    k_ref,
    v_ref,
    q_hbm,
    dq_ref,
    fresh_ref,
    ck_hbm,
    cv_hbm,
    out_ref,
    dec_ref,
    slots,
    q_ref,
    peak_ref,
    total_ref,
    acc_ref,
    bias_ref,
    dbias_ref,
    ck,
    cv,
    cst,
    rx,
    ring_send,
    ring_recv,
    sib_send,
    sib_recv,
    tp_send,
    tp_recv,
    cache_sem,
    q_sem,
):
    tok = q_ref.shape[0]
    half_len = tok // 2
    hd = k_ref.shape[1] // HD
    heads = hd * GROUP
    rows = ck.shape[0]
    cache_dev = ck.shape[1]
    per_row = dq_ref.shape[1] // rows
    n_chip = n_ctx // 2
    half = n_chip // 2

    me = lax.axis_index("ctx")
    tp = lax.axis_index("tp")
    chip, core = lax.div(me, 2), lax.rem(me, 2)
    sibling = me + 1 - 2 * core
    line, along = lax.rem(chip, 2), lax.div(chip, 2)
    place = along + line * (n_chip - 1 - 2 * along)

    def chip_at(position):
        position = lax.rem(position + 2 * n_chip, n_chip)
        far = lax.div(position, half)
        return 2 * (position + far * (n_chip - 1 - 2 * position)) + far

    def owner(position):
        return chip_at(position) * 2 + core

    def sib_owner(position):
        return chip_at(position) * 2 + 1 - core

    right, left = owner(place + 1), owner(place - 1)

    q_copy = pltpu.make_async_copy(q_hbm, q_ref, q_sem)
    q_copy.start()
    cache_copies = []
    for r in range(rows):
        pair = []
        for which, (src, dst) in enumerate(((ck_hbm, ck), (cv_hbm, cv))):
            copy = pltpu.make_async_copy(src.at[r], dst.at[r], cache_sem.at[r, which])
            copy.start()
            pair.append(copy)
        cache_copies.append(pair)

    slots[me, 0:tok, :] = k_ref[...]
    slots[me, tok + META : 2 * tok + META, :] = v_ref[...]
    mark = lax.broadcasted_iota(jnp.int32, (META, hd * HD), 0)
    near = lax.broadcasted_iota(jnp.int32, (META, hd * HD), 1) < half_len
    marks = jnp.where(
        mark == 0,
        jnp.where(near, pos_ref[0], pos_ref[1]),
        jnp.where(near, dest_ref[0, 0], dest_ref[1, 0]),
    )
    slots[me, tok : tok + META, :] = marks.astype(jnp.float32).astype(jnp.bfloat16)

    barrier = pltpu.get_barrier_semaphore()
    for other in (right, left, sibling):
        pl.semaphore_signal(
            barrier, inc=1, device_id={"ctx": other}, device_id_type=pl.DeviceIdType.MESH
        )
    for d in range(1, n_tp):
        pl.semaphore_signal(
            barrier,
            inc=1,
            device_id={"tp": lax.rem(tp + d, n_tp)},
            device_id_type=pl.DeviceIdType.MESH,
        )
    pl.semaphore_wait(barrier, 3 + n_tp - 1)

    pieces = (pl.ds(0, tok + META), pl.ds(tok + META, tok))
    sent = []

    def ring_copy(way, step, piece, slot):
        ref = slots.at[slot, pieces[piece]]
        return pltpu.make_async_remote_copy(
            src_ref=ref,
            dst_ref=ref,
            send_sem=ring_send.at[way, step, piece],
            recv_sem=ring_recv.at[way, step, piece],
            device_id={"ctx": left if way else right},
            device_id_type=pl.DeviceIdType.MESH,
        )

    def sib_copy(way, step, piece, slot):
        ref = slots.at[slot, pieces[piece]]
        return pltpu.make_async_remote_copy(
            src_ref=ref,
            dst_ref=ref,
            send_sem=sib_send.at[way, step, piece],
            recv_sem=sib_recv.at[way, step, piece],
            device_id={"ctx": sibling},
            device_id_type=pl.DeviceIdType.MESH,
        )

    def start(copy):
        copy.start()
        sent.append(copy)

    def ways_of(step, piece):
        return (0, 1) if step < half else (piece,)

    def arrive(step, piece):
        slot = [owner(place - step), owner(place + step)]
        for way in ways_of(step, piece):
            ring_copy(way, step, piece, slot[way]).wait_recv()
            if step < half and way in ways_of(step + 1, piece):
                start(ring_copy(way, step + 1, piece, slot[way]))
            start(sib_copy(way, step, piece, slot[way]))

    def sib_arrive(step):
        slot = [sib_owner(place - step), sib_owner(place + step)]
        for piece in (0, 1):
            for way in ways_of(step, piece) if step else (0,):
                sib_copy(way, step, piece, slot[way]).wait_recv()

    def blocks_of(step):
        if step == 0:
            return [slots.at[me], slots.at[sibling]]
        if step == half:
            return [slots.at[owner(place + step)], slots.at[sib_owner(place + step)]]
        return [slots.at[o(place + way * step)] for o in (owner, sib_owner) for way in (-1, 1)]

    for piece in (0, 1):
        start(ring_copy(0, 1, piece, me))
        start(ring_copy(1, 1, piece, me))
        start(sib_copy(0, 0, piece, me))

    row = lax.broadcasted_iota(jnp.int32, (tok, HD), 0)
    lane = lax.broadcasted_iota(jnp.int32, (tok, HD), 1)
    own_pos = jnp.where(row < half_len, pos_ref[0], pos_ref[1]) * half_len + lax.rem(row, half_len)
    own_pos = own_pos.astype(jnp.float32)
    lane_off = lax.rem(lane, half_len).astype(jnp.float32)
    me_f = me.astype(jnp.float32)

    def chunk(step, between):
        first, last = step == 0, step == half
        blocks = blocks_of(step)
        for c, block in enumerate(blocks):
            meta = block[tok : tok + META, 0:HD].astype(jnp.float32)
            key_pos = meta[0:1, :] * float(half_len) + lane_off
            bias_ref[c] = jnp.where(key_pos <= own_pos, 0.0, FILL)
            dbias_ref[c] = jnp.where(jnp.broadcast_to(meta[1:2, :], (tok, HD)) == me_f, 0.0, FILL)

        def keys_values(k):
            keys = jnp.concatenate([b[0:tok, lanes(k)] for b in blocks], axis=0)
            values = jnp.concatenate([b[tok + META : 2 * tok + META, lanes(k)] for b in blocks], axis=0)
            return keys, values

        def body(i, _):
            base = i * HEADS_STEP
            keys, values = keys_values(lax.div(base, GROUP))
            queries = jnp.concatenate([q_ref[:, lanes(base + j)] for j in range(HEADS_STEP)], axis=0)
            scores = lax.dot_general(queries, keys, NT, preferred_element_type=jnp.float32)
            weights, totals, fades = [], [], []
            for j in range(HEADS_STEP):
                old = None if first else peak_ref[base + j]
                peak, fade, total, weight = softmax_tile(
                    scores[j * tok : (j + 1) * tok], lambda c: bias_ref[c], old
                )
                if not first:
                    total = total + total_ref[base + j] * fade
                if not last:
                    peak_ref[base + j] = peak
                    total_ref[base + j] = total
                weights.append(weight)
                totals.append(total)
                fades.append(fade)
            mixed = jnp.dot(
                jnp.concatenate(weights, axis=0), values, preferred_element_type=jnp.float32
            )
            for j in range(HEADS_STEP):
                acc = mixed[j * tok : (j + 1) * tok]
                if not first:
                    acc = acc + acc_ref[base + j] * fades[j]
                if last:
                    whole = jnp.sum(totals[j], axis=-1, keepdims=True)
                    out_ref[:, lanes(base + j)] = (acc / whole).astype(jnp.bfloat16)
                else:
                    acc_ref[base + j] = acc
            return 0

        turns = heads // HEADS_STEP
        if between is None:
            lax.fori_loop(0, turns, body, 0)
        else:
            lax.fori_loop(0, turns // 2, body, 0)
            between()
            lax.fori_loop(turns // 2, turns, body, 0)

        def dec_body(k, _):
            keys, values = keys_values(k)
            dec_step(k, keys, values, lambda c: dbias_ref[c], False)
            return 0

        lax.fori_loop(0, hd, dec_body, 0, unroll=True)

    def dec_step(k, keys, values, bias, first):
        at = heads + k
        scores = lax.dot_general(
            dq_ref[tp * hd + k], keys, NT, preferred_element_type=jnp.float32
        )
        old = None if first else peak_ref[at]
        peak, fade, total, weight = softmax_tile(scores, bias, old)
        acc = jnp.dot(weight, values, preferred_element_type=jnp.float32)
        if not first:
            total = total + total_ref[at] * fade
            acc = acc + acc_ref[at] * fade
        peak_ref[at] = peak
        total_ref[at] = total
        acc_ref[at] = acc

    drow = lax.broadcasted_iota(jnp.int32, (rows * per_row, HD), 0)
    dlane = lax.broadcasted_iota(jnp.int32, (rows * per_row, HD), 1)
    steps = per_row // GROUP
    fresh_live = (lax.div(drow, per_row) == lax.div(dlane, steps)) & (
        lax.rem(dlane, steps) <= lax.rem(drow, steps)
    )
    dbias_ref[0] = jnp.where(fresh_live, 0.0, FILL)

    def fresh_body(k, _):
        dec_step(k, fresh_ref[0, :, lanes(k)], fresh_ref[1, :, lanes(k)], lambda c: dbias_ref[0], True)
        return 0

    lax.fori_loop(0, hd, fresh_body, 0, unroll=True)

    q_copy.wait()
    sib_arrive(0)
    chunk(0, None)
    arrive(1, 0)

    crow = lax.broadcasted_iota(jnp.int32, (per_row, HD), 1)
    for pair in cache_copies:
        for copy in pair:
            copy.wait()

    def cache_body(k, _):
        for r in range(rows):
            span = slice(r * per_row, (r + 1) * per_row)
            scores = lax.dot_general(
                dq_ref[k, span, :], ck[r, :, lanes(k)], NT, preferred_element_type=jnp.float32
            )
            limit = len_ref[r] - tp * cache_dev
            peak, _, total, weight = softmax_tile(
                scores, lambda c: jnp.where(crow + c * HD < limit, 0.0, FILL), None
            )
            acc = jnp.dot(weight, cv[r, :, lanes(k)], preferred_element_type=jnp.float32)
            whole = jnp.broadcast_to(jnp.sum(total, axis=-1, keepdims=True), total.shape)
            cst[k, 0, span, :] = acc
            cst[k, 1, span, :] = jnp.where(crow < HD // 2, peak, whole)
        return 0

    lax.fori_loop(0, KVH // 2, cache_body, 0)
    arrive(1, 1)
    lax.fori_loop(KVH // 2, KVH, cache_body, 0)

    def tp_copy(d):
        other = lax.rem(tp + d, n_tp)
        return pltpu.make_async_remote_copy(
            src_ref=cst.at[pl.ds(other * hd, hd)],
            dst_ref=rx.at[d],
            send_sem=tp_send.at[d],
            recv_sem=tp_recv.at[d],
            device_id={"tp": other},
            device_id_type=pl.DeviceIdType.MESH,
        )

    tp_copies = [tp_copy(d) for d in range(1, n_tp)]
    for copy in tp_copies:
        copy.start()

    for step in range(1, half):
        sib_arrive(step)

        def between():
            arrive(step + 1, 0)
            if step + 1 == half:
                arrive(half, 1)

        chunk(step, between)
        if step + 1 < half:
            arrive(step + 1, 1)
    sib_arrive(half)
    chunk(half, None)

    for copy in tp_copies:
        copy.wait_recv()

    def final_body(k, _):
        at = heads + k
        peak, acc = peak_ref[at], acc_ref[at]
        whole = jnp.broadcast_to(jnp.sum(total_ref[at], axis=-1, keepdims=True), acc.shape)
        for d in range(n_tp):
            if d == 0:
                part, stats = cst[tp * hd + k, 0], cst[tp * hd + k, 1]
            else:
                part, stats = rx[d, k, 0], rx[d, k, 1]
            far_peak = jnp.broadcast_to(stats[:, 0:1], acc.shape)
            far_whole = jnp.broadcast_to(stats[:, HD // 2 : HD // 2 + 1], acc.shape)
            top = jnp.maximum(peak, far_peak)
            fade, far_fade = jnp.exp2(peak - top), jnp.exp2(far_peak - top)
            whole = whole * fade + far_whole * far_fade
            acc = acc * fade + part * far_fade
            peak = top
        dec_ref[k] = (acc / whole).astype(jnp.bfloat16)
        return 0

    lax.fori_loop(0, hd, final_body, 0, unroll=True)
    for copy in sent:
        copy.wait_send()
    for copy in tp_copies:
        copy.wait_send()


def per_device(
    n_ctx,
    n_tp,
    pre_queries,
    pre_keys,
    pre_values,
    block_pos,
    block_dest,
    dec_queries,
    new_keys,
    new_values,
    cache_keys,
    cache_values,
    cache_len,
):
    tok, width = pre_keys.shape
    hd = width // HD
    rows, steps = dec_queries.shape[:2]
    cache_dev = cache_keys.shape[1]
    dec_all = rows * steps * GROUP
    half = n_ctx // 4

    dq = dec_queries.reshape(rows, steps, KVH, GROUP, HD).transpose(2, 0, 3, 1, 4)
    dq = dq.reshape(KVH, dec_all, HD)
    fresh = jnp.stack([new_keys, new_values]).reshape(2, rows * steps, width)
    fresh = jnp.pad(fresh, ((0, 0), (0, HD - rows * steps), (0, 0)))

    vmem = pl.BlockSpec(memory_space=pltpu.VMEM)
    smem = pl.BlockSpec(memory_space=pltpu.SMEM)
    hbm = pl.BlockSpec(memory_space=pl.ANY)
    states = hd * GROUP + hd
    out, dec = pl.pallas_call(
        functools.partial(kernel, n_ctx, n_tp),
        out_shape=(
            jax.ShapeDtypeStruct((tok, hd * GROUP * HD), jnp.bfloat16),
            jax.ShapeDtypeStruct((hd, dec_all, HD), jnp.bfloat16),
        ),
        in_specs=[smem, smem, smem, vmem, vmem, hbm, vmem, vmem, hbm, hbm],
        out_specs=(vmem, vmem),
        scratch_shapes=[
            pltpu.VMEM((n_ctx, 2 * tok + META, width), jnp.bfloat16),
            pltpu.VMEM(pre_queries.shape, jnp.bfloat16),
            pltpu.VMEM((states, tok, HD), jnp.float32),
            pltpu.VMEM((states, tok, HD), jnp.float32),
            pltpu.VMEM((states, tok, HD), jnp.float32),
            pltpu.VMEM((4, tok, HD), jnp.float32),
            pltpu.VMEM((4, dec_all, HD), jnp.float32),
            pltpu.VMEM((rows, cache_dev, KVH * HD), jnp.bfloat16),
            pltpu.VMEM((rows, cache_dev, KVH * HD), jnp.bfloat16),
            pltpu.VMEM((KVH, 2, dec_all, HD), jnp.float32),
            pltpu.VMEM((n_tp, hd, 2, dec_all, HD), jnp.float32),
            pltpu.SemaphoreType.DMA((2, half + 1, 2)),
            pltpu.SemaphoreType.DMA((2, half + 1, 2)),
            pltpu.SemaphoreType.DMA((2, half + 1, 2)),
            pltpu.SemaphoreType.DMA((2, half + 1, 2)),
            pltpu.SemaphoreType.DMA((n_tp,)),
            pltpu.SemaphoreType.DMA((n_tp,)),
            pltpu.SemaphoreType.DMA((rows, 2)),
            pltpu.SemaphoreType.DMA,
        ],
        compiler_params=pltpu.CompilerParams(
            collective_id=0, has_side_effects=True, vmem_limit_bytes=56 * 1024 * 1024
        ),
    )(
        block_pos,
        block_dest,
        cache_len,
        pre_keys,
        pre_values,
        pre_queries,
        dq,
        fresh,
        cache_keys,
        cache_values,
    )
    dec = dec.reshape(hd, rows, GROUP, steps, HD).transpose(1, 3, 0, 2, 4)
    return out, dec.reshape(rows, steps, hd * GROUP * HD)


def solution(mesh):
    placed = (
        P("ctx", "tp"),
        P("ctx", "tp"),
        P("ctx", "tp"),
        P("ctx"),
        P("ctx", None),
        P("ctx", None, None),
        P("ctx", None, "tp"),
        P("ctx", None, "tp"),
        P("ctx", "tp", None),
        P("ctx", "tp", None),
        P("ctx"),
    )
    return jax.shard_map(
        functools.partial(per_device, mesh.shape["ctx"], mesh.shape["tp"]),
        mesh=mesh,
        in_specs=placed,
        out_specs=(P("ctx", "tp"), P("ctx", None, "tp")),
        check_vma=False,
    )
```
